768 devices in a mesh: dp: 12 (over z), hidden: 64 (over y, x, core).
Axes of the slice: x: 4, y: 8, z: 12, core: 2. Of those that a mesh axis runs over, the one named last changes fastest.
Arguments:
- tokens: bfloat16 [384, 4096], P('dp', 'hidden'), may hold values from -6 to 6
- grad_out: bfloat16 [384, 4096], P('dp', 'hidden'), may hold values from -6 to 6
- routes: int32 [384, 2], P('dp'), may hold values from 0 to 5, all different within a row; in each aligned block of 32 rows (0 to 31, 32 to 63, ...) at most 20 rows name the same one
- probs: bfloat16 [384, 2], P('dp'), may hold values from 0.099609375 to 0.8984375
- gate_weight: bfloat16 [86016, 4096], P(('dp', 'hidden')), may hold values from -0.09375 to 0.09375
- up_weight: bfloat16 [86016, 4096], P(('dp', 'hidden')), may hold values from -0.09375 to 0.09375
- down_weight: bfloat16 [86016, 4096], P(('dp', 'hidden')), may hold values from -0.0625 to 0.0625
Outputs:
- grad_tokens: bfloat16 [384, 4096], P('dp', 'hidden')
- grad_probs: float32 [384, 2], P('dp')
- grad_gate: bfloat16 [86016, 4096], P(('dp', 'hidden'))
- grad_up: bfloat16 [86016, 4096], P(('dp', 'hidden'))
The draws below stay inside these ranges and needn't reach their ends.
Inputs may be any that keep to these rules, and one draw needn't show every extreme that they name: `routes`: A token's two experts differ. Among the 32 tokens of one index of dp no expert is named more than 20 times, a bound that some block reaches.
All inputs are finite; a program needn't handle non-finite values.
Results may differ from the reference program's by a relative error of at most 0.0049.
Values may be sent and summed in bfloat16 or wider, within the bound.
No kernel may reach another device: no remote copies, remote signals or barrier semaphores. Data moves between devices by JAX's collectives and lax.ppermute only.
A program may use at most 128 MiB of HBM per device.

```python
import math
import jax
import jax.numpy as jnp
import numpy as np

D = 4096
FB = 7168
TOK_DEV = 32
CAP = 20
EXPERTS = 6
TOKENS = 384
N_DP = 12


def block_levels(key, dims, cuts, smallest, high):
    gain = 1.0
    for position, blocks in cuts:
        steps = jax.random.uniform(jax.random.fold_in(jax.random.fold_in(key, 6), position), (blocks,), jnp.float32, smallest / len(cuts), high / len(cuts))
        gain = gain * jnp.repeat(jnp.exp(steps), dims[position] // blocks).reshape((-1,) + (1,) * (len(dims) - 1 - position))
    return gain


def assign_block(key, own, number, rows, count, top, limit, slope):
    order = jax.random.permutation(key, count)
    heavy_load, usual = portions_of(count, rows * top, limit, slope, True), portions_of(count, rows * top, limit, slope, False)
    places = jnp.arange(count)

    def named(tallies, turn):
        used = int((tallies > 0).sum())
        fixed = max(1, used // 4)
        passed = fixed + (places - fixed + turn * (used - fixed)) % max(1, count - fixed)
        return jnp.zeros((count,), jnp.int32).at[order[jnp.where(places < fixed, places, passed)]].set(jnp.asarray(tallies, jnp.int32))

    tallies = jnp.where(number % 4 == 0, named(heavy_load, number // 4), named(usual, number - number // 4 - 1))
    mixed = jax.random.permutation(jax.random.fold_in(own, 3), count)
    source_of, receiver = mixed[0:count // 2 * 2:2], mixed[1:count // 2 * 2:2]
    slack = jnp.minimum(tallies[source_of] - 1, limit - tallies[receiver]) // 2
    slack = jnp.where((source_of == order[0]) | (receiver == order[0]) | (tallies[receiver] == 0), 0, jnp.maximum(slack, 0))
    passed = jax.random.randint(jax.random.fold_in(own, 4), (count // 2,), 0, 1 << 20) % (slack + 1)
    tallies = tallies.at[source_of].add(-passed).at[receiver].add(passed)
    members = jnp.searchsorted(jnp.cumsum(tallies), jnp.arange(rows * top), side="right").astype(jnp.int32)
    grid = members.reshape(top, rows).T
    grid = grid[jax.random.permutation(jax.random.fold_in(own, 1), rows)]
    turn = jax.random.randint(jax.random.fold_in(own, 2), (rows, 1), 0, top)
    return jnp.take_along_axis(grid, (jnp.arange(top)[None, :] + turn) % top, axis=1)


def portions_of(amount, total, bound, slope, full):
    portions = [(1 << 20) // math.isqrt(rank ** slope) + 1 for rank in range(1, amount + 1)]
    largest = bound if full else min(bound, max(-(-total // amount), total * portions[0] // sum(portions)))
    least = 1 if total - largest >= amount - 1 else 0
    given, surplus = [largest] + [least] * (amount - 1), total - largest - least * (amount - 1)
    while surplus > 0:
        free = [i for i in range(1, amount) if given[i] < largest] or [i for i in range(1, amount) if given[i] < bound]
        pool, budget = sum([portions[i] for i in free]), surplus
        for i in free:
            extra = min(bound - given[i], max(1, budget * portions[i] // pool), surplus)
            given[i] = given[i] + extra
            surplus = surplus - extra
    return np.array(given)


def normal_values(key, shape, scale, bound, pieces=(), held_as=jnp.bfloat16):
    entries = scale * jax.random.normal(key, shape, jnp.float32)
    if pieces:
        entries = entries * block_levels(key, shape, pieces, -0.22, 0.18)
    return jnp.clip(entries, -bound, bound).astype(held_as)


def setup_inputs(seed: int = 0) -> dict:
    key_list = jax.random.split(jax.random.key(seed), 8)
    tokens = normal_values(key_list[0], (TOKENS, D), 1.0, 6.0, ((0, 12), (1, 64)))
    grad_out = normal_values(key_list[1], (TOKENS, D), 1.0, 6.0, ((0, 12), (1, 64)))
    routes_keys = jax.random.split(jax.random.fold_in(key_list[2], 1), TOKENS // TOK_DEV)
    routes_turns = jax.random.permutation(jax.random.fold_in(key_list[2], 3), TOKENS // TOK_DEV)
    routes = jax.vmap(lambda own, number: assign_block(jax.random.fold_in(key_list[2], 2), own, number, TOK_DEV, EXPERTS, 2, CAP, 2))(routes_keys, routes_turns).reshape((TOKENS, 2))
    probs = jnp.clip(0.099609375 + 0.7988281 * jax.random.uniform(key_list[3], (TOKENS, 2), jnp.float32) ** block_levels(key_list[3], (TOKENS, 2), ((0, 12),), -0.2, 0.2), 0.099609375, 0.8984375).astype(jnp.bfloat16)
    gate_weight = normal_values(key_list[4], (N_DP * FB, D), D ** -0.5, 0.09375, ((0, 768),))
    up_weight = normal_values(key_list[5], (N_DP * FB, D), D ** -0.5, 0.09375, ((0, 768),))
    down_weight = normal_values(key_list[6], (N_DP * FB, D), FB ** -0.5, 0.0625, ((0, 768),))
    return dict(tokens=tokens, grad_out=grad_out, routes=routes, probs=probs, gate_weight=gate_weight, up_weight=up_weight, down_weight=down_weight)


def reference(tokens, grad_out, routes, probs, gate_weight, up_weight, down_weight):
    large_count = N_DP // 6
    weights_f = probs.astype(jnp.float32)
    grad_total = jnp.zeros((TOKENS, D), jnp.float32)
    grad_router = jnp.zeros((TOKENS, 2), jnp.float32)
    gate_grads = []
    up_grads = []
    for block_index in range(N_DP):
        if block_index < 4 * large_count:
            expert_id = block_index // 4
        else:
            expert_id = block_index - 3 * large_count
        first = block_index * FB
        gate_rows = gate_weight[first:first + FB]
        up_rows = up_weight[first:first + FB]
        down_rows = down_weight[first:first + FB]
        matched = routes == expert_id
        block_prob = jnp.sum(jnp.where(matched, weights_f, 0.0), axis=1)
        gate_pre = jnp.dot(tokens, gate_rows.T, preferred_element_type=jnp.float32)
        up_pre = jnp.dot(tokens, up_rows.T, preferred_element_type=jnp.float32)
        back_pre = jnp.dot(grad_out, down_rows.T, preferred_element_type=jnp.float32)
        sigmoid_gate = jax.nn.sigmoid(gate_pre)
        silu_gate = gate_pre * sigmoid_gate
        router_part = jnp.sum(silu_gate * up_pre * back_pre, axis=1)
        scaled = block_prob[:, None] * back_pre
        grad_gate_pre = (scaled * up_pre * sigmoid_gate * (1.0 + gate_pre * (1.0 - sigmoid_gate))).astype(jnp.bfloat16)
        grad_up_pre = (scaled * silu_gate).astype(jnp.bfloat16)
        gate_grads.append(jnp.dot(grad_gate_pre.T, tokens, preferred_element_type=jnp.float32).astype(jnp.bfloat16))
        up_grads.append(jnp.dot(grad_up_pre.T, tokens, preferred_element_type=jnp.float32).astype(jnp.bfloat16))
        grad_total = grad_total + jnp.dot(grad_gate_pre, gate_rows, preferred_element_type=jnp.float32)
        grad_total = grad_total + jnp.dot(grad_up_pre, up_rows, preferred_element_type=jnp.float32)
        grad_router = grad_router + jnp.where(matched, router_part[:, None], 0.0)
    return (grad_total.astype(jnp.bfloat16), grad_router, jnp.concatenate(gate_grads, axis=0), jnp.concatenate(up_grads, axis=0))
```

```python
import jax
import jax.numpy as jnp
from jax import lax
from jax.experimental import pallas as pl
from jax.experimental.pallas import tpu as pltpu
from jax.sharding import Mesh, PartitionSpec as P

DP = 12
CAP = 20
SLOTS = 256
ROWS = 24
BACK = 16
BF = jnp.bfloat16
F32 = jnp.float32
VMEM = pl.BlockSpec(memory_space=pltpu.VMEM)
PLANE = ("yl", "x")
FAR = ("dp", "yh")


def iota(shape, dim):
    return lax.broadcasted_iota(jnp.int32, shape, dim)


def by24(r):
    return (r * 171) >> 12


def by20(s):
    return (s * 205) >> 12


def owner_of(j):
    return jnp.where(j < 8, j >> 2, j - 6)


def dot(a, b, ca, cb, precision=None):
    return lax.dot_general(
        a, b, (((ca,), (cb,)), ((), ())), preferred_element_type=F32, precision=precision
    )


def one_hot(mask):
    return jnp.where(mask, 1.0, 0.0)


def select_kernel(routes, probs, tokens_hbm, grads_hbm, out, tokens, grads, sems):
    copies = [
        pltpu.make_async_copy(tokens_hbm, tokens, sems.at[0]),
        pltpu.make_async_copy(grads_hbm, grads, sems.at[1]),
    ]
    for a in copies:
        a.start()
    rows = DP * ROWS
    r = iota((rows, 32), 0)
    j = by24(r)
    c = r - ROWS * j
    owner = owner_of(j)
    first = routes[0:1, :] == owner
    second = routes[1:2, :] == owner
    hit = one_hot(first | second)
    earlier = one_hot(iota((32, 32), 0) < iota((32, 32), 1)).astype(BF)
    rank = dot(hit.astype(BF), earlier, 1, 0)
    chosen = hit * one_hot(rank == c.astype(F32))
    p = probs[...].astype(F32)
    weight = jnp.sum(chosen * jnp.where(first, p[0:1, :], p[1:2, :]), axis=1, keepdims=True)
    for a in copies:
        a.wait()
    values = jnp.concatenate([tokens[...].astype(F32), grads[...].astype(F32)], axis=1)
    picked = dot(chosen.astype(BF), values.astype(BF), 1, 0)
    rl = iota((rows, 128), 0)
    at_lane = one_hot(rl - ROWS * by24(rl) == iota((rows, 128), 1))
    ra, rb = iota((rows, rows), 0), iota((rows, rows), 1)
    ja = by24(ra)
    gather = one_hot((ra - ROWS * ja == CAP) & (ja == by24(rb)))
    picked += dot(gather.astype(BF), (weight * at_lane).astype(BF), 1, 0)
    block = picked.reshape(DP, ROWS, 128).astype(BF)
    for k in range(4):
        out[:, k] = block


def spread_kernel(recv, out, prob, held):
    rows = DP * ROWS

    @pl.when(pl.program_id(0) == 0)
    def _():
        r, s = iota((rows, SLOTS), 0), iota((rows, SLOTS), 1)
        i = by20(s)
        used = s < DP * CAP
        place = one_hot((r == ROWS * i + (s - CAP * i)) & used).astype(BF)
        for k in range(4):
            block = recv[:, k].astype(F32).reshape(rows, 128).astype(BF)
            held[k] = dot(block, place, 0, 0).astype(BF)
        block = recv[:, 0].astype(F32).reshape(rows, 128).astype(BF)
        lane, sl = iota((128, SLOTS), 0), iota((128, SLOTS), 1)
        fan = one_hot(lane == sl - CAP * by20(sl)).astype(BF)
        fanned = dot(block, fan, 1, 0)
        prob[...] = jnp.sum(
            jnp.where((r == ROWS * i + CAP) & used, fanned, 0.0), axis=0, keepdims=True
        )

    out[0] = held[...]


def place_copies(core, mine, other, held, sems):
    copies = []
    for k in range(8):
        for n, src in enumerate((mine, other)):
            slot = core if n == 0 else 1 - core
            copies.append(
                pltpu.make_async_copy(
                    src.at[k, :, pl.ds(0, 64), :], held.at[:, k, slot], sems.at[2 * k + n]
                )
            )
    return copies


def split(v):
    high = v.astype(BF).astype(F32)
    return high, v - high


def two_rows(v):
    high, low = split(v)
    n = iota((16, SLOTS), 0)
    return jnp.where(n == 0, high, jnp.where(n == 1, low, 0.0)).astype(BF)


def hidden_part(w, x, k):
    at = pl.ds(256 * k, 256)
    tokens = x[k, :, 0:64, :].reshape(256, SLOTS)
    grads = x[k, :, 64:128, :].reshape(256, SLOTS)
    return dot(w[0:224, at], tokens, 1, 0), dot(w[224:336, at], grads, 1, 0)


def own_kernel(core_ref, mine, wg, wu, wd, w_own, w_other, part, w, sems):
    core = core_ref[0]
    copies = []
    for n, src in enumerate((wg, wu, wd)):
        for q in range(4):
            at = pl.ds(1024 * q, 1024)
            dst = w.at[pl.ds(112 * n, 112), at]
            copies.append(pltpu.make_async_copy(src.at[:, at], dst, sems.at[4 * n + q]))
    for a in copies:
        a.start()
    for a in copies:
        a.wait()
    both = jnp.zeros((224, SLOTS), F32)
    back = jnp.zeros((112, SLOTS), F32)
    for k in range(8):
        blocks = [w[:, (yh * 8 + k) * 128 : (yh * 8 + k + 1) * 128] for yh in range(4)]
        low = jnp.concatenate([v[:, 0:64] for v in blocks], axis=1)
        high = jnp.concatenate([v[:, 64:128] for v in blocks], axis=1)
        at = pl.ds(256 * k, 256)
        w_own[:, at] = jnp.where(core == 0, low, high)
        w_other[:, at] = jnp.where(core == 0, high, low)
        b, r = hidden_part(w_own, mine, k)
        both += b
        back += r
    part[0:224] = both
    part[224:336] = back


def main_kernel(other, part, prob, w_other, send, pre, terms):
    both, back = part[0:224], part[224:336]
    for k in range(8):
        b, r = hidden_part(w_other, other, k)
        both += b
        back += r
    gate, up = both[0:112], both[112:224]
    sig = jax.nn.sigmoid(gate)
    silu = gate * sig
    router = two_rows(jnp.sum(silu * up * back, axis=0, keepdims=True))
    scaled = prob[...] * back
    d_gate = (scaled * up * sig * (1.0 + gate * (1.0 - sig))).astype(BF)
    d_up = (scaled * silu).astype(BF)
    grads = jnp.concatenate([d_gate, d_up], axis=0)
    pre[...] = grads
    terms[...] = router
    for k in range(8):
        send[k, 0:256] = dot(w_other[0:224, pl.ds(256 * k, 256)], grads, 0, 0).astype(BF)
        send[k, 256:272] = router


def keep_kernel(w_own, pre, keep):
    for k in range(8):
        keep[k] = dot(w_own[0:224, pl.ds(256 * k, 256)], pre[...], 0, 0)


def weight_kernel(core_ref, mine, other, pre, out_gate, out_up, xt, xsem):
    core = core_ref[0]
    copies = place_copies(core, mine, other, xt, xsem)
    for a in copies:
        a.start()
    for k in range(8):
        copies[2 * k].wait()
        copies[2 * k + 1].wait()
        part = dot(pre[...], xt[:, k].reshape(512, SLOTS), 1, 1).astype(BF)
        for yh in range(4):
            at = pl.ds((yh * 8 + k) * 128, 128)
            out_gate[:, at] = part[0:112, yh * 128 : (yh + 1) * 128]
            out_up[:, at] = part[112:224, yh * 128 : (yh + 1) * 128]


def add_kernel(keep, own_terms, swapped, out):
    out[0, 0:256] = (keep[0] + swapped[0, 0:256].astype(F32)).astype(BF)
    terms = own_terms[...].astype(F32) + swapped[0, 256:272].astype(F32)
    out[0, 256:272] = two_rows(jnp.sum(terms, axis=0, keepdims=True))


def return_kernel(recv, out):
    rows = DP * BACK
    total = recv[0, 0:256].astype(F32)
    terms = recv[0, 256:272].astype(F32)
    for k in range(1, 8):
        total += recv[k, 0:256].astype(F32)
        terms += recv[k, 256:272].astype(F32)
    high, low = split(jnp.sum(terms, axis=0, keepdims=True))
    r, s = iota((rows, SLOTS), 0), iota((rows, SLOTS), 1)
    i, c = r >> 4, r & 15
    in_block = (by20(s) == i) & (s < DP * CAP)
    slot = s - CAP * i
    left = one_hot(in_block & (slot == c) & (c < 10)).astype(BF)
    right = one_hot(in_block & (slot == c + 10) & (c < 10)).astype(BF)
    spread = jnp.where(in_block & (c == 10), high, jnp.where(in_block & (c == 11), low, 0.0))
    sl, lane = iota((SLOTS, 128), 0), iota((SLOTS, 128), 1)
    fan = one_hot(sl - CAP * by20(sl) == lane).astype(BF)
    terms_part = dot(spread.astype(BF), fan, 1, 0)
    empty = jnp.zeros((64, SLOTS), BF)
    for yh in range(4):
        block = total[yh * 64 : (yh + 1) * 64].astype(BF)
        part = terms_part + dot(left, jnp.concatenate([block, empty], axis=0), 1, 1)
        part += dot(right, jnp.concatenate([empty, block], axis=0), 1, 1)
        out[:, yh] = part.reshape(DP, BACK, 128).astype(BF)


def combine_kernel(routes, recv, grad_tokens, grad_probs):
    cols = DP * 4 * BACK
    eye = one_hot(iota((32, 32), 0) == iota((32, 32), 1))
    place = dot(eye.astype(BF), routes[...].astype(F32).astype(BF), 1, 1)
    first, second = place[:, 0:1], place[:, 1:2]
    r = iota((32, cols), 1)
    c = (r & 15).astype(F32)
    owner = owner_of(r >> 6).astype(F32)
    hit = one_hot((first == owner) | (second == owner))
    before = one_hot(iota((32, 32), 1) < iota((32, 32), 0)).astype(BF)
    rank = dot(before, hit.astype(BF), 1, 0)
    paired = hit * one_hot(c < 10.0)
    chosen = jnp.concatenate(
        [paired * one_hot(rank == c), paired * one_hot(rank == c + 10.0)], axis=0
    )
    rows = recv[...].reshape(cols, 128)
    both = dot(chosen.astype(BF), rows, 1, 0)
    grad_tokens[...] = (both[0:32, 0:64] + both[32:64, 64:128]).astype(BF)
    lane = iota((32, 128), 1).astype(F32)
    sums = [jnp.zeros((32, 128), F32), jnp.zeros((32, 128), F32)]
    for j in range(DP):
        terms = jnp.sum(recv[j].astype(F32), axis=0)
        term = terms[10:11] + terms[11:12]
        owner_j = float(j // 4 if j < 8 else j - 6)
        here = jnp.where(rank[:, 64 * j : 64 * j + 1] == lane, term, 0.0)
        sums[0] += jnp.where(first == owner_j, here, 0.0)
        sums[1] += jnp.where(second == owner_j, here, 0.0)
    ones = jnp.ones((8, 128), F32)
    for n in range(2):
        row = dot(ones, sums[n], 1, 1, lax.Precision.HIGHEST)
        grad_probs[n : n + 1, :] = row[0:1, :]


def params():
    return pltpu.CompilerParams(vmem_limit_bytes=40 * 1024 * 1024)


def shape(dims, dtype):
    return jax.ShapeDtypeStruct(dims, dtype)


def body(tokens, grad_out, routes, probs, gate_weight, up_weight, down_weight):
    any_space = pl.BlockSpec(memory_space=pl.ANY)
    smem = pl.BlockSpec(memory_space=pltpu.SMEM)
    core = lax.axis_index("core").astype(jnp.int32).reshape(1)
    routes_t = routes.T
    picked = pl.pallas_call(
        select_kernel,
        out_shape=shape((DP, 4, ROWS, 128), BF),
        in_specs=[VMEM, VMEM, any_space, any_space],
        out_specs=VMEM,
        scratch_shapes=[
            pltpu.VMEM((32, 64), BF),
            pltpu.VMEM((32, 64), BF),
            pltpu.SemaphoreType.DMA((2,)),
        ],
        compiler_params=params(),
        name="select_rows",
    )(routes_t, probs.T, tokens, grad_out)
    got = lax.all_to_all(picked.reshape(DP * 4, ROWS, 128), FAR, 0, 0, tiled=True)
    spread, prob = pl.pallas_call(
        spread_kernel,
        grid=(8,),
        out_shape=(shape((8, 4, 128, SLOTS), BF), shape((1, SLOTS), F32)),
        in_specs=[pl.BlockSpec((DP, 4, ROWS, 128), lambda n: (0, 0, 0, 0))],
        out_specs=(
            pl.BlockSpec((1, 4, 128, SLOTS), lambda n: (n, 0, 0, 0)),
            pl.BlockSpec((1, SLOTS), lambda n: (0, 0)),
        ),
        scratch_shapes=[pltpu.VMEM((4, 128, SLOTS), BF)],
        compiler_params=params(),
        name="spread_rows",
    )(got.reshape(DP, 4, ROWS, 128))
    mine = lax.all_to_all(spread, PLANE, 0, 0, tiled=True)
    swap = [(0, 1), (1, 0)]
    other = lax.ppermute(mine, "core", swap)
    held = pltpu.VMEM((4, 8, 2, 64, SLOTS), BF)
    w_own, w_other, part = pl.pallas_call(
        own_kernel,
        out_shape=(
            shape((336, 2048), BF),
            shape((336, 2048), BF),
            shape((336, SLOTS), F32),
        ),
        in_specs=[smem, VMEM] + [any_space] * 3,
        out_specs=(VMEM,) * 3,
        scratch_shapes=[pltpu.VMEM((336, 4096), BF), pltpu.SemaphoreType.DMA((12,))],
        compiler_params=params(),
        cost_estimate=pl.CostEstimate(
            flops=360_000_000, bytes_accessed=8_000_000, transcendentals=0
        ),
        name="own_features",
    )(core, mine, gate_weight, up_weight, down_weight)
    send, pre, terms = pl.pallas_call(
        main_kernel,
        out_shape=(shape((8, 272, SLOTS), BF), shape((224, SLOTS), BF), shape((16, SLOTS), BF)),
        in_specs=[VMEM] * 4,
        out_specs=(VMEM,) * 3,
        compiler_params=params(),
        cost_estimate=pl.CostEstimate(
            flops=600_000_000, bytes_accessed=5_000_000, transcendentals=30_000
        ),
        name="hidden_and_input_grads",
    )(other, part, prob, w_other)
    swapped = lax.ppermute(send, "core", swap)
    keep = pl.pallas_call(
        keep_kernel,
        out_shape=shape((8, 256, SLOTS), F32),
        in_specs=[VMEM] * 2,
        out_specs=VMEM,
        compiler_params=params(),
        cost_estimate=pl.CostEstimate(
            flops=240_000_000, bytes_accessed=3_000_000, transcendentals=0
        ),
        name="input_grads_kept",
    )(w_own, pre)
    grad_gate, grad_up = pl.pallas_call(
        weight_kernel,
        out_shape=(shape((112, 4096), BF),) * 2,
        in_specs=[smem, any_space, any_space, VMEM],
        out_specs=(VMEM,) * 2,
        scratch_shapes=[held, pltpu.SemaphoreType.DMA((16,))],
        compiler_params=params(),
        cost_estimate=pl.CostEstimate(
            flops=480_000_000, bytes_accessed=4_000_000, transcendentals=0
        ),
        name="weight_grads",
    )(core, mine, other, pre)
    piece = pl.BlockSpec((1, 272, SLOTS), lambda n: (n, 0, 0))
    summed = pl.pallas_call(
        add_kernel,
        grid=(8,),
        out_shape=shape((8, 272, SLOTS), BF),
        in_specs=[
            pl.BlockSpec((1, 256, SLOTS), lambda n: (n, 0, 0)),
            pl.BlockSpec((16, SLOTS), lambda n: (0, 0)),
            piece,
        ],
        out_specs=piece,
        compiler_params=params(),
        name="add_cores",
    )(keep, terms, swapped)
    parts = lax.all_to_all(summed, PLANE, 0, 0, tiled=True)
    back = pl.pallas_call(
        return_kernel,
        out_shape=shape((DP, 4, BACK, 128), BF),
        in_specs=[VMEM],
        out_specs=VMEM,
        compiler_params=params(),
        name="return_rows",
    )(parts)
    home = lax.all_to_all(back.reshape(DP * 4, BACK, 128), FAR, 0, 0, tiled=True)
    grad_tokens, grad_probs = pl.pallas_call(
        combine_kernel,
        out_shape=(shape((32, 64), BF), shape((2, 32), F32)),
        in_specs=[VMEM] * 2,
        out_specs=(VMEM,) * 2,
        compiler_params=params(),
        name="combine",
    )(routes_t, home.reshape(DP, 4, BACK, 128))
    return grad_tokens, grad_probs.T, grad_gate, grad_up


def solution(mesh):
    fine = Mesh(mesh.devices.reshape(DP, 4, 2, 4, 2), ("dp", "yh", "yl", "x", "core"))
    hidden = ("yh", "yl", "x", "core")
    rows = P(("dp",) + hidden, None)
    placed = (P("dp", hidden), P("dp", hidden), P("dp", None), P("dp", None), rows, rows, rows)
    return jax.shard_map(
        body,
        mesh=fine,
        in_specs=placed,
        out_specs=(P("dp", hidden), P("dp", None), rows, rows),
        check_vma=False,
    )
```

```python
import jax
import jax.numpy as jnp
from jax import lax
from jax.experimental import pallas as pl
from jax.experimental.pallas import tpu as pltpu
from jax.sharding import Mesh, PartitionSpec as P

DP = 12
CAP = 20
SLOTS = 256
ROWS = 24
BACK = 16
BF = jnp.bfloat16
F32 = jnp.float32
VMEM = pl.BlockSpec(memory_space=pltpu.VMEM)
PLANE = ("yl", "x")
FAR = ("dp", "yh")


def iota(shape, dim):
    return lax.broadcasted_iota(jnp.int32, shape, dim)


def by24(r):
    return (r * 171) >> 12


def by20(s):
    return (s * 205) >> 12


def owner_of(j):
    return jnp.where(j < 8, j >> 2, j - 6)


def dot(a, b, ca, cb, precision=None):
    return lax.dot_general(
        a, b, (((ca,), (cb,)), ((), ())), preferred_element_type=F32, precision=precision
    )


def one_hot(mask):
    return jnp.where(mask, 1.0, 0.0)


def select_kernel(routes, probs, tokens, grads, out):
    rows = DP * ROWS
    r = iota((rows, 32), 0)
    j = by24(r)
    c = r - ROWS * j
    owner = owner_of(j)
    first = routes[0:1, :] == owner
    second = routes[1:2, :] == owner
    hit = one_hot(first | second)
    earlier = one_hot(iota((32, 32), 0) < iota((32, 32), 1)).astype(BF)
    rank = dot(hit.astype(BF), earlier, 1, 0)
    chosen = hit * one_hot(rank == c.astype(F32))
    p = probs[...].astype(F32)
    weight = jnp.sum(chosen * jnp.where(first, p[0:1, :], p[1:2, :]), axis=1, keepdims=True)
    values = jnp.concatenate([tokens[...].astype(F32), grads[...].astype(F32)], axis=1)
    picked = dot(chosen.astype(BF), values.astype(BF), 1, 0)
    rl = iota((rows, 128), 0)
    at_lane = one_hot(rl - ROWS * by24(rl) == iota((rows, 128), 1))
    ra, rb = iota((rows, rows), 0), iota((rows, rows), 1)
    ja = by24(ra)
    gather = one_hot((ra - ROWS * ja == CAP) & (ja == by24(rb)))
    picked += dot(gather.astype(BF), (weight * at_lane).astype(BF), 1, 0)
    block = picked.reshape(DP, ROWS, 128).astype(BF)
    for k in range(4):
        out[:, k] = block


def spread_kernel(recv, out, prob, held, sems):
    rows = DP * ROWS
    r, s = iota((rows, SLOTS), 0), iota((rows, SLOTS), 1)
    i = by20(s)
    used = s < DP * CAP
    place = one_hot((r == ROWS * i + (s - CAP * i)) & used).astype(BF)
    blocks = [recv[:, k].astype(F32).reshape(rows, 128).astype(BF) for k in range(4)]
    copies = []
    for k in range(4):
        held[k] = dot(blocks[k], place, 0, 0).astype(BF)
        for n in range(8):
            copy = pltpu.make_async_copy(held.at[k], out.at[n, k], sems.at[8 * k + n])
            copy.start()
            copies.append(copy)
    lane, sl = iota((128, SLOTS), 0), iota((128, SLOTS), 1)
    fan = one_hot(lane == sl - CAP * by20(sl)).astype(BF)
    fanned = dot(blocks[0], fan, 1, 0)
    prob[...] = jnp.sum(
        jnp.where((r == ROWS * i + CAP) & used, fanned, 0.0), axis=0, keepdims=True
    )
    for copy in copies:
        copy.wait()


def place_copies(core, mine, other, held, sems):
    copies = []
    for k in range(8):
        for n, src in enumerate((mine, other)):
            slot = core if n == 0 else 1 - core
            copies.append(
                pltpu.make_async_copy(
                    src.at[k, :, pl.ds(0, 64), :], held.at[:, k, slot], sems.at[2 * k + n]
                )
            )
    return copies


def split(v):
    high = v.astype(BF).astype(F32)
    return high, v - high


def two_rows(v):
    high, low = split(v)
    n = iota((16, SLOTS), 0)
    return jnp.where(n == 0, high, jnp.where(n == 1, low, 0.0)).astype(BF)


def sort_kernel(core_ref, wg, wu, wd, w_own, w_away, w, sems):
    core = core_ref[0]
    copies = []
    for n, src in enumerate((wg, wu, wd)):
        for q in range(4):
            at = pl.ds(1024 * q, 1024)
            dst = w.at[pl.ds(112 * n, 112), at]
            copies.append(pltpu.make_async_copy(src.at[:, at], dst, sems.at[4 * n + q]))
    for a in copies:
        a.start()
    for a in copies:
        a.wait()
    for k in range(8):
        blocks = [w[:, (yh * 8 + k) * 128 : (yh * 8 + k + 1) * 128] for yh in range(4)]
        low = jnp.concatenate([v[:, 0:64] for v in blocks], axis=1)
        high = jnp.concatenate([v[:, 64:128] for v in blocks], axis=1)
        at = pl.ds(256 * k, 256)
        w_own[:, at] = jnp.where(core == 0, low, high)
        w_away[:, at] = jnp.where(core == 0, high, low)


def hold_kernel(w, out):
    out[...] = w[...]


def features_kernel(mine, w, part):
    both = jnp.zeros((224, SLOTS), F32)
    back = jnp.zeros((112, SLOTS), F32)
    for k in range(8):
        at = pl.ds(256 * k, 256)
        both += dot(w[0:224, at], mine[k, :, 0:64, :].reshape(256, SLOTS), 1, 0)
        back += dot(w[224:336, at], mine[k, :, 64:128, :].reshape(256, SLOTS), 1, 0)
    part[0:224] = both
    part[224:336] = back


def hidden_kernel(own, got, prob, pre):
    gate = own[0:112] + got[0:112]
    up = own[112:224] + got[112:224]
    back = own[224:336] + got[224:336]
    sig = jax.nn.sigmoid(gate)
    silu = gate * sig
    scaled = prob[...] * back
    pre[0:112] = (scaled * up * sig * (1.0 + gate * (1.0 - sig))).astype(BF)
    pre[112:224] = (scaled * silu).astype(BF)
    pre[224:240] = two_rows(jnp.sum(silu * up * back, axis=0, keepdims=True))


def keep_kernel(w_own, pre, keep):
    for k in range(8):
        keep[k] = dot(w_own[0:224, pl.ds(256 * k, 256)], pre[0:224], 0, 0)


def sum_kernel(keep, w_near, pre, pre_near, out):
    terms = pre[224:240].astype(F32) + pre_near[224:240].astype(F32)
    router = two_rows(jnp.sum(terms, axis=0, keepdims=True))
    for k in range(8):
        part = dot(w_near[0:224, pl.ds(256 * k, 256)], pre_near[0:224], 0, 0)
        out[k, 0:256] = (keep[k] + part).astype(BF)
        out[k, 256:272] = router


def weight_kernel(core_ref, mine, other, pre, out_gate, out_up, done, xt, xsem):
    core = core_ref[0]
    copies = place_copies(core, mine, other, xt, xsem)
    for a in copies:
        a.start()
    for k in range(8):
        copies[2 * k].wait()
        copies[2 * k + 1].wait()
        part = dot(pre[0:224], xt[:, k].reshape(512, SLOTS), 1, 1).astype(BF)
        for yh in range(4):
            at = pl.ds((yh * 8 + k) * 128, 128)
            out_gate[:, at] = part[0:112, yh * 128 : (yh + 1) * 128]
            out_up[:, at] = part[112:224, yh * 128 : (yh + 1) * 128]
    done[...] = jnp.zeros((8, 128), F32)


def return_kernel(recv, out, held, sems):
    rows = DP * BACK
    total = recv[0, 0:256].astype(F32)
    terms = recv[0, 256:272].astype(F32)
    for k in range(1, 8):
        total += recv[k, 0:256].astype(F32)
        terms += recv[k, 256:272].astype(F32)
    high, low = split(jnp.sum(terms, axis=0, keepdims=True))
    r, s = iota((rows, SLOTS), 0), iota((rows, SLOTS), 1)
    i, c = r >> 4, r & 15
    in_block = (by20(s) == i) & (s < DP * CAP)
    slot = s - CAP * i
    left = one_hot(in_block & (slot == c) & (c < 10)).astype(BF)
    right = one_hot(in_block & (slot == c + 10) & (c < 10)).astype(BF)
    spread = jnp.where(in_block & (c == 10), high, jnp.where(in_block & (c == 11), low, 0.0))
    sl, lane = iota((SLOTS, 128), 0), iota((SLOTS, 128), 1)
    fan = one_hot(sl - CAP * by20(sl) == lane).astype(BF)
    terms_part = dot(spread.astype(BF), fan, 1, 0)
    empty = jnp.zeros((64, SLOTS), BF)
    copies = []
    for yh in range(4):
        block = total[yh * 64 : (yh + 1) * 64].astype(BF)
        part = terms_part + dot(left, jnp.concatenate([block, empty], axis=0), 1, 1)
        part += dot(right, jnp.concatenate([empty, block], axis=0), 1, 1)
        held[yh] = part.reshape(DP, BACK, 128).astype(BF)
        copies.append(pltpu.make_async_copy(held.at[yh], out.at[:, yh], sems.at[yh]))
        copies[yh].start()
    for copy in copies:
        copy.wait()


def mask_kernel(routes, after, chosen, masks):
    cols = DP * 4 * BACK
    eye = one_hot(iota((32, 32), 0) == iota((32, 32), 1))
    place = dot(eye.astype(BF), routes[...].astype(F32).astype(BF), 1, 1)
    first, second = place[:, 0:1], place[:, 1:2]
    r = iota((32, cols), 1)
    c = (r & 15).astype(F32)
    owner = owner_of(r >> 6).astype(F32)
    hit = one_hot((first == owner) | (second == owner))
    before = one_hot(iota((32, 32), 1) < iota((32, 32), 0)).astype(BF)
    rank = dot(before, hit.astype(BF), 1, 0)
    paired = hit * one_hot(c < 10.0)
    both = jnp.concatenate(
        [paired * one_hot(rank == c), paired * one_hot(rank == c + 10.0)], axis=0
    )
    chosen[...] = both.astype(BF)
    lane = iota((32, 128), 1).astype(F32)
    for j in range(DP):
        owner_j = float(j // 4 if j < 8 else j - 6)
        here = one_hot(rank[:, 64 * j : 64 * j + 1] == lane)
        masks[0, j] = jnp.where(first == owner_j, here, 0.0)
        masks[1, j] = jnp.where(second == owner_j, here, 0.0)


def combine_kernel(chosen, masks, recv, grad_tokens, grad_probs):
    both = dot(chosen[...], recv[...].reshape(DP * 4 * BACK, 128), 1, 0)
    grad_tokens[...] = (both[0:32, 0:64] + both[32:64, 64:128]).astype(BF)
    sums = [jnp.zeros((32, 128), F32), jnp.zeros((32, 128), F32)]
    for j in range(DP):
        terms = jnp.sum(recv[j].astype(F32), axis=0)
        term = terms[10:11] + terms[11:12]
        for n in range(2):
            sums[n] += jnp.where(masks[n, j] > 0.5, term, 0.0)
    ones = jnp.ones((8, 128), F32)
    for n in range(2):
        row = dot(ones, sums[n], 1, 1, lax.Precision.HIGHEST)
        grad_probs[n : n + 1, :] = row[0:1, :]


def params(mib=16):
    return pltpu.CompilerParams(vmem_limit_bytes=mib * 1024 * 1024)


def shape(dims, dtype):
    return jax.ShapeDtypeStruct(dims, dtype)


def body(tokens, grad_out, routes, probs, gate_weight, up_weight, down_weight):
    any_space = pl.BlockSpec(memory_space=pl.ANY)
    smem = pl.BlockSpec(memory_space=pltpu.SMEM)
    core = lax.axis_index("core").astype(jnp.int32).reshape(1)
    routes_t = routes.T
    whole = [pl.BlockSpec(dims, lambda n: (0, 0)) for dims in ((2, 32), (32, 64))]
    picked = pl.pallas_call(
        select_kernel,
        grid=(1,),
        out_shape=pltpu.VMEM((DP, 4, ROWS, 128), BF),
        in_specs=[whole[0], whole[0], whole[1], whole[1]],
        out_specs=pl.BlockSpec((DP, 4, ROWS, 128), lambda n: (0, 0, 0, 0)),
        compiler_params=params(60),
        name="select_rows",
    )(routes_t, probs.T, tokens, grad_out)
    swap = [(0, 1), (1, 0)]
    w_own, w_away = pl.pallas_call(
        sort_kernel,
        out_shape=(pltpu.VMEM((336, 2048), BF),) * 2,
        in_specs=[smem] + [pl.BlockSpec(memory_space=pltpu.HBM)] * 3,
        out_specs=(VMEM,) * 2,
        scratch_shapes=[pltpu.VMEM((336, 4096), BF), pltpu.SemaphoreType.DMA((12,))],
        compiler_params=params(),
        cost_estimate=pl.CostEstimate(
            flops=0, bytes_accessed=8_000_000, transcendentals=0
        ),
        name="sort_columns",
    )(core, gate_weight, up_weight, down_weight)
    w_near = pl.pallas_call(
        hold_kernel,
        out_shape=pltpu.VMEM((336, 2048), BF),
        in_specs=[VMEM],
        out_specs=VMEM,
        compiler_params=params(),
        name="hold_columns",
    )(lax.ppermute(w_away, "core", swap))
    got = lax.all_to_all(picked.reshape(DP * 4, ROWS, 128), FAR, 0, 0, tiled=True)
    spread, prob = pl.pallas_call(
        spread_kernel,
        out_shape=(pltpu.HBM((8, 4, 128, SLOTS), BF), shape((1, SLOTS), F32)),
        in_specs=[VMEM],
        out_specs=(any_space, VMEM),
        scratch_shapes=[pltpu.VMEM((4, 128, SLOTS), BF), pltpu.SemaphoreType.DMA((32,))],
        compiler_params=params(),
        name="spread_rows",
    )(got.reshape(DP, 4, ROWS, 128))
    mine = lax.all_to_all(spread, PLANE, 0, 0, tiled=True)
    away, part = [
        pl.pallas_call(
            features_kernel,
            out_shape=shape((336, SLOTS), F32),
            in_specs=[VMEM] * 2,
            out_specs=VMEM,
            compiler_params=params(),
            cost_estimate=pl.CostEstimate(
                flops=360_000_000, bytes_accessed=4_000_000, transcendentals=0
            ),
            name=name,
        )(mine, w)
        for name, w in (("features_away", w_near), ("features_own", w_own))
    ]
    got_part = lax.ppermute(away, "core", swap)
    pre = pl.pallas_call(
        hidden_kernel,
        out_shape=shape((240, SLOTS), BF),
        in_specs=[VMEM] * 3,
        out_specs=VMEM,
        compiler_params=params(),
        name="hidden_units",
    )(part, got_part, prob)
    pre_near = lax.ppermute(pre, "core", swap)
    keep = pl.pallas_call(
        keep_kernel,
        out_shape=shape((8, 256, SLOTS), F32),
        in_specs=[VMEM] * 2,
        out_specs=VMEM,
        compiler_params=params(),
        cost_estimate=pl.CostEstimate(
            flops=240_000_000, bytes_accessed=3_000_000, transcendentals=0
        ),
        name="input_grads_own",
    )(w_own, pre)
    summed = pl.pallas_call(
        sum_kernel,
        out_shape=shape((8, 272, SLOTS), BF),
        in_specs=[VMEM] * 4,
        out_specs=VMEM,
        compiler_params=params(),
        name="input_grads_both",
    )(keep, w_near, pre, pre_near)
    parts = lax.all_to_all(summed, PLANE, 0, 0, tiled=True)
    back = pl.pallas_call(
        return_kernel,
        out_shape=pltpu.HBM((DP, 4, BACK, 128), BF),
        in_specs=[VMEM],
        out_specs=any_space,
        scratch_shapes=[pltpu.VMEM((4, DP, BACK, 128), BF), pltpu.SemaphoreType.DMA((4,))],
        compiler_params=params(),
        name="return_rows",
    )(parts)
    late, back = lax.optimization_barrier((mine, back))
    other = lax.ppermute(late, "core", swap)
    grad_gate, grad_up, done = pl.pallas_call(
        weight_kernel,
        out_shape=(shape((112, 4096), BF),) * 2 + (shape((8, 128), F32),),
        in_specs=[smem, any_space, any_space, VMEM],
        out_specs=(VMEM,) * 3,
        scratch_shapes=[
            pltpu.VMEM((4, 8, 2, 64, SLOTS), BF),
            pltpu.SemaphoreType.DMA((16,)),
        ],
        compiler_params=params(),
        cost_estimate=pl.CostEstimate(
            flops=1_000, bytes_accessed=1_000, transcendentals=0
        ),
        name="weight_grads",
    )(core, late, other, pre)
    home = lax.all_to_all(back.reshape(DP * 4, BACK, 128), FAR, 0, 0, tiled=True)
    chosen, masks = pl.pallas_call(
        mask_kernel,
        out_shape=(shape((64, DP * 4 * BACK), BF), shape((2, DP, 32, 128), F32)),
        in_specs=[VMEM] * 2,
        out_specs=(VMEM,) * 2,
        compiler_params=params(),
        name="masks",
    )(routes_t, done)
    grad_tokens, grad_probs = pl.pallas_call(
        combine_kernel,
        out_shape=(shape((32, 64), BF), shape((2, 32), F32)),
        in_specs=[VMEM] * 3,
        out_specs=(VMEM,) * 2,
        compiler_params=params(),
        name="combine",
    )(chosen, masks, home.reshape(DP, 4, BACK, 128))
    return grad_tokens, grad_probs.T, grad_gate, grad_up


def solution(mesh):
    fine = Mesh(mesh.devices.reshape(DP, 4, 2, 4, 2), ("dp", "yh", "yl", "x", "core"))
    hidden = ("yh", "yl", "x", "core")
    rows = P(("dp",) + hidden, None)
    placed = (P("dp", hidden), P("dp", hidden), P("dp", None), P("dp", None), rows, rows, rows)
    return jax.shard_map(
        body,
        mesh=fine,
        in_specs=placed,
        out_specs=(P("dp", hidden), P("dp", None), rows, rows),
        check_vma=False,
    )
```

```python
import jax
import jax.numpy as jnp
from jax import lax
from jax.experimental import pallas as pl
from jax.experimental.pallas import tpu as pltpu
from jax.sharding import Mesh, PartitionSpec as P

DP = 12
CAP = 20
SLOTS = 256
ROWS = 24
BACK = 16
BF = jnp.bfloat16
F32 = jnp.float32
VMEM = pl.BlockSpec(memory_space=pltpu.VMEM)
PLANE = ("yl", "x")
FAR = ("dp", "yh")


def iota(shape, dim):
    return lax.broadcasted_iota(jnp.int32, shape, dim)


def by24(r):
    return (r * 171) >> 12


def by20(s):
    return (s * 205) >> 12


def owner_of(j):
    return jnp.where(j < 8, j >> 2, j - 6)


def dot(a, b, ca, cb, precision=None):
    return lax.dot_general(
        a, b, (((ca,), (cb,)), ((), ())), preferred_element_type=F32, precision=precision
    )


def one_hot(mask):
    return jnp.where(mask, 1.0, 0.0)


def select_kernel(routes, probs, tokens, grads, out):
    rows = DP * ROWS
    r = iota((rows, 32), 0)
    j = by24(r)
    c = r - ROWS * j
    owner = owner_of(j)
    first = routes[0:1, :] == owner
    second = routes[1:2, :] == owner
    hit = one_hot(first | second)
    earlier = one_hot(iota((32, 32), 0) < iota((32, 32), 1)).astype(BF)
    rank = dot(hit.astype(BF), earlier, 1, 0)
    chosen = hit * one_hot(rank == c.astype(F32))
    p = probs[...].astype(F32)
    weight = jnp.sum(chosen * jnp.where(first, p[0:1, :], p[1:2, :]), axis=1, keepdims=True)
    values = jnp.concatenate([tokens[...].astype(F32), grads[...].astype(F32)], axis=1)
    picked = dot(chosen.astype(BF), values.astype(BF), 1, 0)
    rl = iota((rows, 128), 0)
    at_lane = one_hot(rl - ROWS * by24(rl) == iota((rows, 128), 1))
    ra, rb = iota((rows, rows), 0), iota((rows, rows), 1)
    ja = by24(ra)
    gather = one_hot((ra - ROWS * ja == CAP) & (ja == by24(rb)))
    picked += dot(gather.astype(BF), (weight * at_lane).astype(BF), 1, 0)
    block = picked.reshape(DP, ROWS, 128).astype(BF)
    for k in range(4):
        out[:, k] = block


def spread_kernel(recv, out, prob, held, sems):
    rows = DP * ROWS
    r, s = iota((rows, SLOTS), 0), iota((rows, SLOTS), 1)
    i = by20(s)
    used = s < DP * CAP
    place = one_hot((r == ROWS * i + (s - CAP * i)) & used).astype(BF)
    blocks = [recv[:, k].astype(F32).reshape(rows, 128).astype(BF) for k in range(4)]
    copies = []
    for k in range(4):
        held[k] = dot(blocks[k], place, 0, 0).astype(BF)
        for n in range(8):
            copy = pltpu.make_async_copy(held.at[k], out.at[n, k], sems.at[8 * k + n])
            copy.start()
            copies.append(copy)
    lane, sl = iota((128, SLOTS), 0), iota((128, SLOTS), 1)
    fan = one_hot(lane == sl - CAP * by20(sl)).astype(BF)
    fanned = dot(blocks[0], fan, 1, 0)
    prob[...] = jnp.sum(
        jnp.where((r == ROWS * i + CAP) & used, fanned, 0.0), axis=0, keepdims=True
    )
    for copy in copies:
        copy.wait()


def place_copies(core, mine, other, held, sems):
    copies = []
    for k in range(8):
        for n, src in enumerate((mine, other)):
            slot = core if n == 0 else 1 - core
            copies.append(
                pltpu.make_async_copy(
                    src.at[k, :, pl.ds(0, 64), :], held.at[:, k, slot], sems.at[2 * k + n]
                )
            )
    return copies


def split(v):
    high = v.astype(BF).astype(F32)
    return high, v - high


def two_rows(v):
    high, low = split(v)
    n = iota((16, SLOTS), 0)
    return jnp.where(n == 0, high, jnp.where(n == 1, low, 0.0)).astype(BF)


def sort_kernel(core_ref, wg, wu, wd, w_own, w_away, w, sems):
    core = core_ref[0]
    copies = []
    for n, src in enumerate((wg, wu, wd)):
        for q in range(4):
            at = pl.ds(1024 * q, 1024)
            dst = w.at[pl.ds(112 * n, 112), at]
            copies.append(pltpu.make_async_copy(src.at[:, at], dst, sems.at[4 * n + q]))
    for a in copies:
        a.start()
    for a in copies:
        a.wait()
    for k in range(8):
        blocks = [w[:, (yh * 8 + k) * 128 : (yh * 8 + k + 1) * 128] for yh in range(4)]
        low = jnp.concatenate([v[:, 0:64] for v in blocks], axis=1)
        high = jnp.concatenate([v[:, 64:128] for v in blocks], axis=1)
        at = pl.ds(256 * k, 256)
        w_own[:, at] = jnp.where(core == 0, low, high)
        w_away[:, at] = jnp.where(core == 0, high, low)


def hold_kernel(w, out):
    out[...] = w[...]


def features_kernel(mine, w, part):
    both = jnp.zeros((224, SLOTS), F32)
    back = jnp.zeros((112, SLOTS), F32)
    for k in range(8):
        at = pl.ds(256 * k, 256)
        both += dot(w[0:224, at], mine[k, :, 0:64, :].reshape(256, SLOTS), 1, 0)
        back += dot(w[224:336, at], mine[k, :, 64:128, :].reshape(256, SLOTS), 1, 0)
    part[0:224] = both
    part[224:336] = back


def hidden_kernel(own, got, prob, pre):
    gate = own[0:112] + got[0:112]
    up = own[112:224] + got[112:224]
    back = own[224:336] + got[224:336]
    sig = jax.nn.sigmoid(gate)
    silu = gate * sig
    scaled = prob[...] * back
    pre[0:112] = (scaled * up * sig * (1.0 + gate * (1.0 - sig))).astype(BF)
    pre[112:224] = (scaled * silu).astype(BF)
    pre[224:240] = two_rows(jnp.sum(silu * up * back, axis=0, keepdims=True))


def keep_kernel(w_own, pre, keep):
    for k in range(8):
        keep[k] = dot(w_own[0:224, pl.ds(256 * k, 256)], pre[0:224], 0, 0)


def sum_kernel(keep, w_near, pre, pre_near, out, held, sems):
    terms = pre[224:240].astype(F32) + pre_near[224:240].astype(F32)
    router = two_rows(jnp.sum(terms, axis=0, keepdims=True))
    copies = []
    for k in range(8):
        part = dot(w_near[0:224, pl.ds(256 * k, 256)], pre_near[0:224], 0, 0)
        held[k, 0:256] = (keep[k] + part).astype(BF)
        held[k, 256:272] = router
        copies.append(pltpu.make_async_copy(held.at[k], out.at[k], sems.at[k]))
        copies[k].start()
    for copy in copies:
        copy.wait()


def weight_kernel(core_ref, mine, other, pre, out_gate, out_up, done, xt, xsem):
    core = core_ref[0]
    copies = place_copies(core, mine, other, xt, xsem)
    for a in copies:
        a.start()
    for k in range(8):
        copies[2 * k].wait()
        copies[2 * k + 1].wait()
        part = dot(pre[0:224], xt[:, k].reshape(512, SLOTS), 1, 1).astype(BF)
        for yh in range(4):
            at = pl.ds((yh * 8 + k) * 128, 128)
            out_gate[:, at] = part[0:112, yh * 128 : (yh + 1) * 128]
            out_up[:, at] = part[112:224, yh * 128 : (yh + 1) * 128]
    done[...] = jnp.zeros((8, 128), F32)


def return_kernel(recv, out, held, sems):
    rows = DP * BACK
    total = recv[0, 0:256].astype(F32)
    terms = recv[0, 256:272].astype(F32)
    for k in range(1, 8):
        total += recv[k, 0:256].astype(F32)
        terms += recv[k, 256:272].astype(F32)
    high, low = split(jnp.sum(terms, axis=0, keepdims=True))
    r, s = iota((rows, SLOTS), 0), iota((rows, SLOTS), 1)
    i, c = r >> 4, r & 15
    in_block = (by20(s) == i) & (s < DP * CAP)
    slot = s - CAP * i
    left = one_hot(in_block & (slot == c) & (c < 10)).astype(BF)
    right = one_hot(in_block & (slot == c + 10) & (c < 10)).astype(BF)
    spread = jnp.where(in_block & (c == 10), high, jnp.where(in_block & (c == 11), low, 0.0))
    sl, lane = iota((SLOTS, 128), 0), iota((SLOTS, 128), 1)
    fan = one_hot(sl - CAP * by20(sl) == lane).astype(BF)
    terms_part = dot(spread.astype(BF), fan, 1, 0)
    empty = jnp.zeros((64, SLOTS), BF)
    copies = []
    for yh in range(4):
        block = total[yh * 64 : (yh + 1) * 64].astype(BF)
        part = terms_part + dot(left, jnp.concatenate([block, empty], axis=0), 1, 1)
        part += dot(right, jnp.concatenate([empty, block], axis=0), 1, 1)
        held[yh] = part.reshape(DP, BACK, 128).astype(BF)
        copies.append(pltpu.make_async_copy(held.at[yh], out.at[:, yh], sems.at[yh]))
        copies[yh].start()
    for copy in copies:
        copy.wait()


def mask_kernel(routes, after, chosen, masks):
    cols = DP * 4 * BACK
    eye = one_hot(iota((32, 32), 0) == iota((32, 32), 1))
    place = dot(eye.astype(BF), routes[...].astype(F32).astype(BF), 1, 1)
    first, second = place[:, 0:1], place[:, 1:2]
    r = iota((32, cols), 1)
    c = (r & 15).astype(F32)
    owner = owner_of(r >> 6).astype(F32)
    hit = one_hot((first == owner) | (second == owner))
    before = one_hot(iota((32, 32), 1) < iota((32, 32), 0)).astype(BF)
    rank = dot(before, hit.astype(BF), 1, 0)
    paired = hit * one_hot(c < 10.0)
    both = jnp.concatenate(
        [paired * one_hot(rank == c), paired * one_hot(rank == c + 10.0)], axis=0
    )
    chosen[...] = both.astype(BF)
    lane = iota((32, 128), 1).astype(F32)
    for j in range(DP):
        owner_j = float(j // 4 if j < 8 else j - 6)
        here = one_hot(rank[:, 64 * j : 64 * j + 1] == lane)
        masks[0, j] = jnp.where(first == owner_j, here, 0.0)
        masks[1, j] = jnp.where(second == owner_j, here, 0.0)


def combine_kernel(chosen, masks, recv, grad_tokens, grad_probs):
    both = dot(chosen[...], recv[...].reshape(DP * 4 * BACK, 128), 1, 0)
    grad_tokens[...] = (both[0:32, 0:64] + both[32:64, 64:128]).astype(BF)
    sums = [jnp.zeros((32, 128), F32), jnp.zeros((32, 128), F32)]
    for j in range(DP):
        terms = jnp.sum(recv[j].astype(F32), axis=0)
        term = terms[10:11] + terms[11:12]
        for n in range(2):
            sums[n] += jnp.where(masks[n, j] > 0.5, term, 0.0)
    ones = jnp.ones((8, 128), F32)
    for n in range(2):
        row = dot(ones, sums[n], 1, 1, lax.Precision.HIGHEST)
        grad_probs[n : n + 1, :] = row[0:1, :]


def params(mib=16):
    return pltpu.CompilerParams(vmem_limit_bytes=mib * 1024 * 1024)


def shape(dims, dtype):
    return jax.ShapeDtypeStruct(dims, dtype)


def body(tokens, grad_out, routes, probs, gate_weight, up_weight, down_weight):
    any_space = pl.BlockSpec(memory_space=pl.ANY)
    smem = pl.BlockSpec(memory_space=pltpu.SMEM)
    core = lax.axis_index("core").astype(jnp.int32).reshape(1)
    routes_t = routes.T
    whole = [pl.BlockSpec(dims, lambda n: (0, 0)) for dims in ((2, 32), (32, 64))]
    picked = pl.pallas_call(
        select_kernel,
        grid=(1,),
        out_shape=pltpu.VMEM((DP, 4, ROWS, 128), BF),
        in_specs=[whole[0], whole[0], whole[1], whole[1]],
        out_specs=pl.BlockSpec((DP, 4, ROWS, 128), lambda n: (0, 0, 0, 0)),
        compiler_params=params(60),
        name="select_rows",
    )(routes_t, probs.T, tokens, grad_out)
    swap = [(0, 1), (1, 0)]
    w_own, w_away = pl.pallas_call(
        sort_kernel,
        out_shape=(pltpu.VMEM((336, 2048), BF),) * 2,
        in_specs=[smem] + [pl.BlockSpec(memory_space=pltpu.HBM)] * 3,
        out_specs=(VMEM,) * 2,
        scratch_shapes=[pltpu.VMEM((336, 4096), BF), pltpu.SemaphoreType.DMA((12,))],
        compiler_params=params(),
        cost_estimate=pl.CostEstimate(
            flops=0, bytes_accessed=8_000_000, transcendentals=0
        ),
        name="sort_columns",
    )(core, gate_weight, up_weight, down_weight)
    w_near = pl.pallas_call(
        hold_kernel,
        out_shape=pltpu.VMEM((336, 2048), BF),
        in_specs=[VMEM],
        out_specs=VMEM,
        compiler_params=params(),
        name="hold_columns",
    )(lax.ppermute(w_away, "core", swap))
    got = lax.all_to_all(picked.reshape(DP * 4, ROWS, 128), FAR, 0, 0, tiled=True)
    spread, prob = pl.pallas_call(
        spread_kernel,
        out_shape=(pltpu.HBM((8, 4, 128, SLOTS), BF), shape((1, SLOTS), F32)),
        in_specs=[VMEM],
        out_specs=(any_space, VMEM),
        scratch_shapes=[pltpu.VMEM((4, 128, SLOTS), BF), pltpu.SemaphoreType.DMA((32,))],
        compiler_params=params(),
        name="spread_rows",
    )(got.reshape(DP, 4, ROWS, 128))
    mine = lax.all_to_all(spread, PLANE, 0, 0, tiled=True)
    away, part = [
        pl.pallas_call(
            features_kernel,
            out_shape=shape((336, SLOTS), F32),
            in_specs=[VMEM] * 2,
            out_specs=VMEM,
            compiler_params=params(),
            cost_estimate=pl.CostEstimate(
                flops=360_000_000, bytes_accessed=4_000_000, transcendentals=0
            ),
            name=name,
        )(mine, w)
        for name, w in (("features_away", w_near), ("features_own", w_own))
    ]
    got_part = lax.ppermute(away, "core", swap)
    pre = pl.pallas_call(
        hidden_kernel,
        out_shape=shape((240, SLOTS), BF),
        in_specs=[VMEM] * 3,
        out_specs=VMEM,
        compiler_params=params(),
        name="hidden_units",
    )(part, got_part, prob)
    pre_near = lax.ppermute(pre, "core", swap)
    keep = pl.pallas_call(
        keep_kernel,
        out_shape=shape((8, 256, SLOTS), F32),
        in_specs=[VMEM] * 2,
        out_specs=VMEM,
        compiler_params=params(),
        cost_estimate=pl.CostEstimate(
            flops=240_000_000, bytes_accessed=3_000_000, transcendentals=0
        ),
        name="input_grads_own",
    )(w_own, pre)
    summed = pl.pallas_call(
        sum_kernel,
        out_shape=pltpu.HBM((8, 272, SLOTS), BF),
        in_specs=[VMEM] * 4,
        out_specs=any_space,
        scratch_shapes=[pltpu.VMEM((8, 272, SLOTS), BF), pltpu.SemaphoreType.DMA((8,))],
        compiler_params=params(),
        name="input_grads_both",
    )(keep, w_near, pre, pre_near)
    parts = lax.all_to_all(summed, PLANE, 0, 0, tiled=True)
    back = pl.pallas_call(
        return_kernel,
        out_shape=pltpu.HBM((DP, 4, BACK, 128), BF),
        in_specs=[VMEM],
        out_specs=any_space,
        scratch_shapes=[pltpu.VMEM((4, DP, BACK, 128), BF), pltpu.SemaphoreType.DMA((4,))],
        compiler_params=params(),
        name="return_rows",
    )(parts)
    other = lax.ppermute(mine, "core", swap)
    grad_gate, grad_up, done = pl.pallas_call(
        weight_kernel,
        out_shape=(shape((112, 4096), BF),) * 2 + (shape((8, 128), F32),),
        in_specs=[smem, any_space, any_space, VMEM],
        out_specs=(VMEM,) * 3,
        scratch_shapes=[
            pltpu.VMEM((4, 8, 2, 64, SLOTS), BF),
            pltpu.SemaphoreType.DMA((16,)),
        ],
        compiler_params=params(),
        cost_estimate=pl.CostEstimate(
            flops=1_000, bytes_accessed=1_000, transcendentals=0
        ),
        name="weight_grads",
    )(core, mine, other, pre)
    home = lax.all_to_all(back.reshape(DP * 4, BACK, 128), FAR, 0, 0, tiled=True)
    chosen, masks = pl.pallas_call(
        mask_kernel,
        out_shape=(shape((64, DP * 4 * BACK), BF), shape((2, DP, 32, 128), F32)),
        in_specs=[VMEM] * 2,
        out_specs=(VMEM,) * 2,
        compiler_params=params(),
        name="masks",
    )(routes_t, done)
    grad_tokens, grad_probs = pl.pallas_call(
        combine_kernel,
        out_shape=(shape((32, 64), BF), shape((2, 32), F32)),
        in_specs=[VMEM] * 3,
        out_specs=(VMEM,) * 2,
        compiler_params=params(),
        name="combine",
    )(chosen, masks, home.reshape(DP, 4, BACK, 128))
    return grad_tokens, grad_probs.T, grad_gate, grad_up


def solution(mesh):
    fine = Mesh(mesh.devices.reshape(DP, 4, 2, 4, 2), ("dp", "yh", "yl", "x", "core"))
    hidden = ("yh", "yl", "x", "core")
    rows = P(("dp",) + hidden, None)
    placed = (P("dp", hidden), P("dp", hidden), P("dp", None), P("dp", None), rows, rows, rows)
    return jax.shard_map(
        body,
        mesh=fine,
        in_specs=placed,
        out_specs=(P("dp", hidden), P("dp", None), rows, rows),
        check_vma=False,
    )
```

```python
import jax
import jax.numpy as jnp
from jax import lax
from jax.experimental import pallas as pl
from jax.experimental.pallas import tpu as pltpu
from jax.sharding import Mesh, PartitionSpec as P

DP = 12
CAP = 20
SLOTS = 256
ROWS = 24
BACK = 16
BF = jnp.bfloat16
F32 = jnp.float32
VMEM = pl.BlockSpec(memory_space=pltpu.VMEM)
PLANE = ("yl", "x")
FAR = ("dp", "yh")


def iota(shape, dim):
    return lax.broadcasted_iota(jnp.int32, shape, dim)


def by24(r):
    return (r * 171) >> 12


def by20(s):
    return (s * 205) >> 12


def owner_of(j):
    return jnp.where(j < 8, j >> 2, j - 6)


def dot(a, b, ca, cb, precision=None):
    return lax.dot_general(
        a, b, (((ca,), (cb,)), ((), ())), preferred_element_type=F32, precision=precision
    )


def one_hot(mask):
    return jnp.where(mask, 1.0, 0.0)


def select_kernel(routes, probs, tokens, grads, out):
    rows = DP * ROWS
    r = iota((rows, 32), 0)
    j = by24(r)
    c = r - ROWS * j
    owner = owner_of(j)
    first = routes[0:1, :] == owner
    second = routes[1:2, :] == owner
    hit = one_hot(first | second)
    earlier = one_hot(iota((32, 32), 0) < iota((32, 32), 1)).astype(BF)
    rank = dot(hit.astype(BF), earlier, 1, 0)
    chosen = hit * one_hot(rank == c.astype(F32))
    p = probs[...].astype(F32)
    weight = jnp.sum(chosen * jnp.where(first, p[0:1, :], p[1:2, :]), axis=1, keepdims=True)
    values = jnp.concatenate([tokens[...].astype(F32), grads[...].astype(F32)], axis=1)
    picked = dot(chosen.astype(BF), values.astype(BF), 1, 0)
    rl = iota((rows, 128), 0)
    at_lane = one_hot(rl - ROWS * by24(rl) == iota((rows, 128), 1))
    ra, rb = iota((rows, rows), 0), iota((rows, rows), 1)
    ja = by24(ra)
    gather = one_hot((ra - ROWS * ja == CAP) & (ja == by24(rb)))
    picked += dot(gather.astype(BF), (weight * at_lane).astype(BF), 1, 0)
    block = picked.reshape(DP, ROWS, 128).astype(BF)
    for k in range(4):
        out[:, k] = block


def spread_kernel(recv, out, prob, held, sems):
    rows = DP * ROWS
    r, s = iota((rows, SLOTS), 0), iota((rows, SLOTS), 1)
    i = by20(s)
    used = s < DP * CAP
    place = one_hot((r == ROWS * i + (s - CAP * i)) & used).astype(BF)
    blocks = [recv[:, k].astype(F32).reshape(rows, 128).astype(BF) for k in range(4)]
    copies = []
    for k in range(4):
        held[k] = dot(blocks[k], place, 0, 0).astype(BF)
        for n in range(8):
            copy = pltpu.make_async_copy(held.at[k], out.at[n, k], sems.at[8 * k + n])
            copy.start()
            copies.append(copy)
    lane, sl = iota((128, SLOTS), 0), iota((128, SLOTS), 1)
    fan = one_hot(lane == sl - CAP * by20(sl)).astype(BF)
    fanned = dot(blocks[0], fan, 1, 0)
    prob[...] = jnp.sum(
        jnp.where((r == ROWS * i + CAP) & used, fanned, 0.0), axis=0, keepdims=True
    )
    for copy in copies:
        copy.wait()


def place_copies(core, mine, other, held, sems):
    copies = []
    for k in range(8):
        for n, src in enumerate((mine, other)):
            slot = core if n == 0 else 1 - core
            copies.append(
                pltpu.make_async_copy(
                    src.at[k, :, pl.ds(0, 64), :], held.at[:, k, slot], sems.at[2 * k + n]
                )
            )
    return copies


def split(v):
    high = v.astype(BF).astype(F32)
    return high, v - high


def two_rows(v):
    high, low = split(v)
    n = iota((16, SLOTS), 0)
    return jnp.where(n == 0, high, jnp.where(n == 1, low, 0.0)).astype(BF)


def sort_kernel(core_ref, wg, wu, wd, w_own, w_away, w, sems):
    core = core_ref[0]
    copies = []
    for n, src in enumerate((wg, wu, wd)):
        for q in range(4):
            at = pl.ds(1024 * q, 1024)
            dst = w.at[pl.ds(112 * n, 112), at]
            copies.append(pltpu.make_async_copy(src.at[:, at], dst, sems.at[4 * n + q]))
    for a in copies:
        a.start()
    for a in copies:
        a.wait()
    for k in range(8):
        blocks = [w[:, (yh * 8 + k) * 128 : (yh * 8 + k + 1) * 128] for yh in range(4)]
        low = jnp.concatenate([v[:, 0:64] for v in blocks], axis=1)
        high = jnp.concatenate([v[:, 64:128] for v in blocks], axis=1)
        at = pl.ds(256 * k, 256)
        w_own[:, at] = jnp.where(core == 0, low, high)
        w_away[:, at] = jnp.where(core == 0, high, low)


def hold_kernel(w, out):
    out[...] = w[...]


def add_features(mine, w, part, first):
    both = jnp.zeros((224, SLOTS), F32)
    back = jnp.zeros((112, SLOTS), F32)
    for k in range(8):
        at = pl.ds(256 * k, 256)
        both += dot(w[0:224, at], mine[k, :, 0:64, :].reshape(256, SLOTS), 1, 0)
        back += dot(w[224:336, at], mine[k, :, 64:128, :].reshape(256, SLOTS), 1, 0)
    part[first : first + 224] = both
    part[first + 224 : first + 336] = back


def near_kernel(mine, w_near, part):
    add_features(mine, w_near, part, 0)


def own_kernel(mine, w_own, near, part):
    part[0:336] = near[...]
    add_features(mine, w_own, part, 336)


def hidden_grads(v, prob):
    gate, up, back = v[0:112], v[112:224], v[224:336]
    sig = jax.nn.sigmoid(gate)
    silu = gate * sig
    scaled = prob * back
    d_gate = (scaled * up * sig * (1.0 + gate * (1.0 - sig))).astype(BF)
    d_up = (scaled * silu).astype(BF)
    router = jnp.sum(silu * up * back, axis=0, keepdims=True)
    return jnp.concatenate([d_gate, d_up], axis=0), router


def grads_kernel(part, got, prob, w_own, w_near, out, pre, held, own_held, sems):
    own, own_terms = hidden_grads(part[336:672] + got[0:336], prob[...])
    near, near_terms = hidden_grads(part[0:336] + got[336:672], prob[...])
    own_held[...] = own
    copies = [pltpu.make_async_copy(own_held, pre, sems.at[8])]
    copies[0].start()
    router = two_rows(own_terms + near_terms)
    both = jnp.concatenate([own, near], axis=0)
    for k in range(8):
        at = pl.ds(256 * k, 256)
        w = jnp.concatenate([w_own[0:224, at], w_near[0:224, at]], axis=0)
        held[k, 0:256] = dot(w, both, 0, 0).astype(BF)
        held[k, 256:272] = router
        copies.append(pltpu.make_async_copy(held.at[k], out.at[k], sems.at[k]))
        copies[k + 1].start()
    for copy in copies:
        copy.wait()


def weight_kernel(core_ref, mine, other, pre, out_gate, out_up, done, xt, xsem):
    core = core_ref[0]
    copies = place_copies(core, mine, other, xt, xsem)
    for a in copies:
        a.start()
    for k in range(8):
        copies[2 * k].wait()
        copies[2 * k + 1].wait()
        part = dot(pre[...], xt[:, k].reshape(512, SLOTS), 1, 1).astype(BF)
        for yh in range(4):
            at = pl.ds((yh * 8 + k) * 128, 128)
            out_gate[:, at] = part[0:112, yh * 128 : (yh + 1) * 128]
            out_up[:, at] = part[112:224, yh * 128 : (yh + 1) * 128]
    done[...] = jnp.zeros((8, 128), F32)


def return_kernel(recv, out, held, sems):
    rows = DP * BACK
    total = recv[0, 0:256].astype(F32)
    terms = recv[0, 256:272].astype(F32)
    for k in range(1, 8):
        total += recv[k, 0:256].astype(F32)
        terms += recv[k, 256:272].astype(F32)
    high, low = split(jnp.sum(terms, axis=0, keepdims=True))
    r, s = iota((rows, SLOTS), 0), iota((rows, SLOTS), 1)
    i, c = r >> 4, r & 15
    in_block = (by20(s) == i) & (s < DP * CAP)
    slot = s - CAP * i
    left = one_hot(in_block & (slot == c) & (c < 10)).astype(BF)
    right = one_hot(in_block & (slot == c + 10) & (c < 10)).astype(BF)
    spread = jnp.where(in_block & (c == 10), high, jnp.where(in_block & (c == 11), low, 0.0))
    sl, lane = iota((SLOTS, 128), 0), iota((SLOTS, 128), 1)
    fan = one_hot(sl - CAP * by20(sl) == lane).astype(BF)
    terms_part = dot(spread.astype(BF), fan, 1, 0)
    empty = jnp.zeros((64, SLOTS), BF)
    copies = []
    for yh in range(4):
        block = total[yh * 64 : (yh + 1) * 64].astype(BF)
        part = terms_part + dot(left, jnp.concatenate([block, empty], axis=0), 1, 1)
        part += dot(right, jnp.concatenate([empty, block], axis=0), 1, 1)
        held[yh] = part.reshape(DP, BACK, 128).astype(BF)
        copies.append(pltpu.make_async_copy(held.at[yh], out.at[:, yh], sems.at[yh]))
        copies[yh].start()
    for copy in copies:
        copy.wait()


def mask_kernel(routes, after, chosen, masks):
    cols = DP * 4 * BACK
    eye = one_hot(iota((32, 32), 0) == iota((32, 32), 1))
    place = dot(eye.astype(BF), routes[...].astype(F32).astype(BF), 1, 1)
    first, second = place[:, 0:1], place[:, 1:2]
    r = iota((32, cols), 1)
    c = (r & 15).astype(F32)
    owner = owner_of(r >> 6).astype(F32)
    hit = one_hot((first == owner) | (second == owner))
    before = one_hot(iota((32, 32), 1) < iota((32, 32), 0)).astype(BF)
    rank = dot(before, hit.astype(BF), 1, 0)
    paired = hit * one_hot(c < 10.0)
    both = jnp.concatenate(
        [paired * one_hot(rank == c), paired * one_hot(rank == c + 10.0)], axis=0
    )
    chosen[...] = both.astype(BF)
    lane = iota((32, 128), 1).astype(F32)
    for j in range(DP):
        owner_j = float(j // 4 if j < 8 else j - 6)
        here = one_hot(rank[:, 64 * j : 64 * j + 1] == lane)
        masks[0, j] = jnp.where(first == owner_j, here, 0.0)
        masks[1, j] = jnp.where(second == owner_j, here, 0.0)


def combine_kernel(chosen, masks, recv, grad_tokens, grad_probs):
    both = dot(chosen[...], recv[...].reshape(DP * 4 * BACK, 128), 1, 0)
    grad_tokens[...] = (both[0:32, 0:64] + both[32:64, 64:128]).astype(BF)
    sums = [jnp.zeros((32, 128), F32), jnp.zeros((32, 128), F32)]
    for j in range(DP):
        terms = jnp.sum(recv[j].astype(F32), axis=0)
        term = terms[10:11] + terms[11:12]
        for n in range(2):
            sums[n] += jnp.where(masks[n, j] > 0.5, term, 0.0)
    ones = jnp.ones((8, 128), F32)
    for n in range(2):
        row = dot(ones, sums[n], 1, 1, lax.Precision.HIGHEST)
        grad_probs[n : n + 1, :] = row[0:1, :]


def params(mib=16):
    return pltpu.CompilerParams(vmem_limit_bytes=mib * 1024 * 1024)


def shape(dims, dtype):
    return jax.ShapeDtypeStruct(dims, dtype)


def body(tokens, grad_out, routes, probs, gate_weight, up_weight, down_weight):
    any_space = pl.BlockSpec(memory_space=pl.ANY)
    smem = pl.BlockSpec(memory_space=pltpu.SMEM)
    core = lax.axis_index("core").astype(jnp.int32).reshape(1)
    routes_t = routes.T
    whole = [pl.BlockSpec(dims, lambda n: (0, 0)) for dims in ((2, 32), (32, 64))]
    picked = pl.pallas_call(
        select_kernel,
        grid=(1,),
        out_shape=pltpu.VMEM((DP, 4, ROWS, 128), BF),
        in_specs=[whole[0], whole[0], whole[1], whole[1]],
        out_specs=pl.BlockSpec((DP, 4, ROWS, 128), lambda n: (0, 0, 0, 0)),
        compiler_params=params(60),
        name="select_rows",
    )(routes_t, probs.T, tokens, grad_out)
    swap = [(0, 1), (1, 0)]
    w_own, w_away = pl.pallas_call(
        sort_kernel,
        out_shape=(pltpu.VMEM((336, 2048), BF),) * 2,
        in_specs=[smem] + [pl.BlockSpec(memory_space=pltpu.HBM)] * 3,
        out_specs=(VMEM,) * 2,
        scratch_shapes=[pltpu.VMEM((336, 4096), BF), pltpu.SemaphoreType.DMA((12,))],
        compiler_params=params(),
        cost_estimate=pl.CostEstimate(
            flops=0, bytes_accessed=8_000_000, transcendentals=0
        ),
        name="sort_columns",
    )(core, gate_weight, up_weight, down_weight)
    w_near = pl.pallas_call(
        hold_kernel,
        out_shape=pltpu.VMEM((336, 2048), BF),
        in_specs=[VMEM],
        out_specs=VMEM,
        compiler_params=params(),
        name="hold_columns",
    )(lax.ppermute(w_away, "core", swap))
    got = lax.all_to_all(picked.reshape(DP * 4, ROWS, 128), FAR, 0, 0, tiled=True)
    spread, prob = pl.pallas_call(
        spread_kernel,
        out_shape=(pltpu.HBM((8, 4, 128, SLOTS), BF), shape((1, SLOTS), F32)),
        in_specs=[VMEM],
        out_specs=(any_space, VMEM),
        scratch_shapes=[pltpu.VMEM((4, 128, SLOTS), BF), pltpu.SemaphoreType.DMA((32,))],
        compiler_params=params(),
        name="spread_rows",
    )(got.reshape(DP, 4, ROWS, 128))
    mine = lax.all_to_all(spread, PLANE, 0, 0, tiled=True)
    near = pl.pallas_call(
        near_kernel,
        out_shape=shape((336, SLOTS), F32),
        in_specs=[VMEM] * 2,
        out_specs=VMEM,
        compiler_params=params(),
        name="features_near",
    )(mine, w_near)
    part = pl.pallas_call(
        own_kernel,
        out_shape=shape((672, SLOTS), F32),
        in_specs=[VMEM] * 3,
        out_specs=VMEM,
        compiler_params=params(),
        name="features_own",
    )(mine, w_own, near)
    got_part = lax.ppermute(part, "core", swap)
    summed, pre = pl.pallas_call(
        grads_kernel,
        out_shape=(pltpu.HBM((8, 272, SLOTS), BF), pltpu.HBM((224, SLOTS), BF)),
        in_specs=[VMEM] * 5,
        out_specs=(any_space, any_space),
        scratch_shapes=[
            pltpu.VMEM((8, 272, SLOTS), BF),
            pltpu.VMEM((224, SLOTS), BF),
            pltpu.SemaphoreType.DMA((9,)),
        ],
        compiler_params=params(),
        name="hidden_and_input_grads",
    )(part, got_part, prob, w_own, w_near)
    parts = lax.all_to_all(summed, PLANE, 0, 0, tiled=True)
    back = pl.pallas_call(
        return_kernel,
        out_shape=pltpu.HBM((DP, 4, BACK, 128), BF),
        in_specs=[VMEM],
        out_specs=any_space,
        scratch_shapes=[pltpu.VMEM((4, DP, BACK, 128), BF), pltpu.SemaphoreType.DMA((4,))],
        compiler_params=params(),
        name="return_rows",
    )(parts)
    other = lax.ppermute(mine, "core", swap)
    grad_gate, grad_up, done = pl.pallas_call(
        weight_kernel,
        out_shape=(shape((112, 4096), BF),) * 2 + (shape((8, 128), F32),),
        in_specs=[smem, any_space, any_space, VMEM],
        out_specs=(VMEM,) * 3,
        scratch_shapes=[
            pltpu.VMEM((4, 8, 2, 64, SLOTS), BF),
            pltpu.SemaphoreType.DMA((16,)),
        ],
        compiler_params=params(),
        cost_estimate=pl.CostEstimate(
            flops=1_000, bytes_accessed=1_000, transcendentals=0
        ),
        name="weight_grads",
    )(core, mine, other, pre)
    home = lax.all_to_all(back.reshape(DP * 4, BACK, 128), FAR, 0, 0, tiled=True)
    chosen, masks = pl.pallas_call(
        mask_kernel,
        out_shape=(shape((64, DP * 4 * BACK), BF), shape((2, DP, 32, 128), F32)),
        in_specs=[VMEM] * 2,
        out_specs=(VMEM,) * 2,
        compiler_params=params(),
        name="masks",
    )(routes_t, done)
    grad_tokens, grad_probs = pl.pallas_call(
        combine_kernel,
        out_shape=(shape((32, 64), BF), shape((2, 32), F32)),
        in_specs=[VMEM] * 3,
        out_specs=(VMEM,) * 2,
        compiler_params=params(),
        name="combine",
    )(chosen, masks, home.reshape(DP, 4, BACK, 128))
    return grad_tokens, grad_probs.T, grad_gate, grad_up


def solution(mesh):
    fine = Mesh(mesh.devices.reshape(DP, 4, 2, 4, 2), ("dp", "yh", "yl", "x", "core"))
    hidden = ("yh", "yl", "x", "core")
    rows = P(("dp",) + hidden, None)
    placed = (P("dp", hidden), P("dp", hidden), P("dp", None), P("dp", None), rows, rows, rows)
    return jax.shard_map(
        body,
        mesh=fine,
        in_specs=placed,
        out_specs=(P("dp", hidden), P("dp", None), rows, rows),
        check_vma=False,
    )
```

```python
import jax
import jax.numpy as jnp
from jax import lax
from jax.experimental import pallas as pl
from jax.experimental.pallas import tpu as pltpu
from jax.sharding import Mesh, PartitionSpec as P

DP = 12
CAP = 20
SLOTS = 256
ROWS = 24
BACK = 16
BF = jnp.bfloat16
F32 = jnp.float32
VMEM = pl.BlockSpec(memory_space=pltpu.VMEM)
PLANE = ("yl", "x")
FAR = ("dp", "yh")


def iota(shape, dim):
    return lax.broadcasted_iota(jnp.int32, shape, dim)


def by24(r):
    return (r * 171) >> 12


def by20(s):
    return (s * 205) >> 12


def owner_of(j):
    return jnp.where(j < 8, j >> 2, j - 6)


def dot(a, b, ca, cb, precision=None):
    return lax.dot_general(
        a, b, (((ca,), (cb,)), ((), ())), preferred_element_type=F32, precision=precision
    )


def one_hot(mask):
    return jnp.where(mask, 1.0, 0.0)


def select_kernel(routes, probs, tokens, grads, out):
    rows = DP * ROWS
    r = iota((rows, 32), 0)
    j = by24(r)
    c = r - ROWS * j
    owner = owner_of(j)
    first = routes[0:1, :] == owner
    second = routes[1:2, :] == owner
    hit = one_hot(first | second)
    earlier = one_hot(iota((32, 32), 0) < iota((32, 32), 1)).astype(BF)
    rank = dot(hit.astype(BF), earlier, 1, 0)
    chosen = hit * one_hot(rank == c.astype(F32))
    p = probs[...].astype(F32)
    weight = jnp.sum(chosen * jnp.where(first, p[0:1, :], p[1:2, :]), axis=1, keepdims=True)
    values = jnp.concatenate([tokens[...].astype(F32), grads[...].astype(F32)], axis=1)
    picked = dot(chosen.astype(BF), values.astype(BF), 1, 0)
    rl = iota((rows, 128), 0)
    at_lane = one_hot(rl - ROWS * by24(rl) == iota((rows, 128), 1))
    weights = jnp.sum((weight * at_lane).reshape(DP, ROWS, 128), axis=1, keepdims=True)
    last = iota((DP, ROWS, 128), 1) == CAP
    block = (picked.reshape(DP, ROWS, 128) + jnp.where(last, weights, 0.0)).astype(BF)
    for k in range(4):
        out[:, k] = block


def spread_kernel(recv, out, prob, held, sems):
    rows = DP * ROWS
    r, s = iota((rows, SLOTS), 0), iota((rows, SLOTS), 1)
    i = by20(s)
    used = s < DP * CAP
    place = one_hot((r == ROWS * i + (s - CAP * i)) & used).astype(BF)
    copies = []
    for k in range(4):
        block = recv[:, k].astype(F32).reshape(rows, 128).astype(BF)
        held[k] = dot(block, place, 0, 0).astype(BF)
        for n in range(8):
            copy = pltpu.make_async_copy(held.at[k], out.at[n, k], sems.at[8 * k + n])
            copy.start()
            copies.append(copy)
    lane, sl = iota((128, SLOTS), 0), iota((128, SLOTS), 1)
    fan = one_hot(lane == sl - CAP * by20(sl)).astype(BF)
    fanned = dot(block, fan, 1, 0)
    prob[...] = jnp.sum(
        jnp.where((r == ROWS * i + CAP) & used, fanned, 0.0), axis=0, keepdims=True
    )
    for copy in copies:
        copy.wait()


def place_copies(core, mine, other, held, sems):
    copies = []
    for k in range(8):
        for n, src in enumerate((mine, other)):
            slot = core if n == 0 else 1 - core
            copies.append(
                pltpu.make_async_copy(
                    src.at[k, :, pl.ds(0, 64), :], held.at[:, k, slot], sems.at[2 * k + n]
                )
            )
    return copies


def split(v):
    high = v.astype(BF).astype(F32)
    return high, v - high


def two_rows(v):
    high, low = split(v)
    n = iota((16, SLOTS), 0)
    return jnp.where(n == 0, high, jnp.where(n == 1, low, 0.0)).astype(BF)


def sort_kernel(core_ref, wg, wu, wd, w_own, w_away, w, sems):
    core = core_ref[0]
    copies = []
    for n, src in enumerate((wg, wu, wd)):
        for q in range(4):
            at = pl.ds(1024 * q, 1024)
            dst = w.at[pl.ds(112 * n, 112), at]
            copies.append(pltpu.make_async_copy(src.at[:, at], dst, sems.at[4 * n + q]))
    for a in copies:
        a.start()
    for a in copies:
        a.wait()
    for k in range(8):
        blocks = [w[:, (yh * 8 + k) * 128 : (yh * 8 + k + 1) * 128] for yh in range(4)]
        low = jnp.concatenate([v[:, 0:64] for v in blocks], axis=1)
        high = jnp.concatenate([v[:, 64:128] for v in blocks], axis=1)
        at = pl.ds(256 * k, 256)
        w_own[:, at] = jnp.where(core == 0, low, high)
        w_away[:, at] = jnp.where(core == 0, high, low)


def hold_kernel(w, out):
    out[...] = w[...]


def add_features(mine, w, part, first):
    both = jnp.zeros((224, SLOTS), F32)
    back = jnp.zeros((112, SLOTS), F32)
    for k in range(8):
        at = pl.ds(256 * k, 256)
        both += dot(w[0:224, at], mine[k, :, 0:64, :].reshape(256, SLOTS), 1, 0)
        back += dot(w[224:336, at], mine[k, :, 64:128, :].reshape(256, SLOTS), 1, 0)
    part[first : first + 224] = both
    part[first + 224 : first + 336] = back


def near_kernel(mine, w_near, part):
    add_features(mine, w_near, part, 0)


def own_kernel(mine, w_own, near, part):
    part[0:336] = near[...]
    add_features(mine, w_own, part, 336)


def hidden_grads(v, prob):
    gate, up, back = v[0:112], v[112:224], v[224:336]
    sig = jax.nn.sigmoid(gate)
    silu = gate * sig
    scaled = prob * back
    d_gate = (scaled * up * sig * (1.0 + gate * (1.0 - sig))).astype(BF)
    d_up = (scaled * silu).astype(BF)
    router = jnp.sum(silu * up * back, axis=0, keepdims=True)
    return jnp.concatenate([d_gate, d_up], axis=0), router


def grads_kernel(part, got, prob, w_own, w_near, out, pre, held, own_held, sems):
    own, own_terms = hidden_grads(part[336:672] + got[0:336], prob[...])
    near, near_terms = hidden_grads(part[0:336] + got[336:672], prob[...])
    own_held[...] = own
    copies = [pltpu.make_async_copy(own_held, pre, sems.at[8])]
    copies[0].start()
    router = two_rows(own_terms + near_terms)
    both = jnp.concatenate([own, near], axis=0)
    for k in range(8):
        at = pl.ds(256 * k, 256)
        w = jnp.concatenate([w_own[0:224, at], w_near[0:224, at]], axis=0)
        held[k, 0:256] = dot(w, both, 0, 0).astype(BF)
        held[k, 256:272] = router
        copies.append(pltpu.make_async_copy(held.at[k], out.at[k], sems.at[k]))
        copies[k + 1].start()
    for copy in copies:
        copy.wait()


def weight_kernel(core_ref, mine, other, pre, out_gate, out_up, done, xt, xsem):
    core = core_ref[0]
    copies = place_copies(core, mine, other, xt, xsem)
    for a in copies:
        a.start()
    for k in range(8):
        copies[2 * k].wait()
        copies[2 * k + 1].wait()
        part = dot(pre[...], xt[:, k].reshape(512, SLOTS), 1, 1).astype(BF)
        for yh in range(4):
            at = pl.ds((yh * 8 + k) * 128, 128)
            out_gate[:, at] = part[0:112, yh * 128 : (yh + 1) * 128]
            out_up[:, at] = part[112:224, yh * 128 : (yh + 1) * 128]
    done[...] = jnp.zeros((8, 128), F32)


def return_kernel(recv, out, held, sems):
    rows = DP * BACK
    total = recv[0, 0:256].astype(F32)
    terms = recv[0, 256:272].astype(F32)
    for k in range(1, 8):
        total += recv[k, 0:256].astype(F32)
        terms += recv[k, 256:272].astype(F32)
    high, low = split(jnp.sum(terms, axis=0, keepdims=True))
    r, s = iota((rows, SLOTS), 0), iota((rows, SLOTS), 1)
    i, c = r >> 4, r & 15
    in_block = (by20(s) == i) & (s < DP * CAP)
    slot = s - CAP * i
    left = one_hot(in_block & (slot == c) & (c < 10)).astype(BF)
    right = one_hot(in_block & (slot == c + 10) & (c < 10)).astype(BF)
    spread = jnp.where(in_block & (c == 10), high, jnp.where(in_block & (c == 11), low, 0.0))
    sl, lane = iota((SLOTS, 128), 0), iota((SLOTS, 128), 1)
    fan = one_hot(sl - CAP * by20(sl) == lane).astype(BF)
    terms_part = dot(spread.astype(BF), fan, 1, 0)
    empty = jnp.zeros((64, SLOTS), BF)
    copies = []
    for yh in range(4):
        block = total[yh * 64 : (yh + 1) * 64].astype(BF)
        part = terms_part + dot(left, jnp.concatenate([block, empty], axis=0), 1, 1)
        part += dot(right, jnp.concatenate([empty, block], axis=0), 1, 1)
        held[yh] = part.reshape(DP, BACK, 128).astype(BF)
        copies.append(pltpu.make_async_copy(held.at[yh], out.at[:, yh], sems.at[yh]))
        copies[yh].start()
    for copy in copies:
        copy.wait()


def mask_kernel(routes, after, chosen, masks):
    cols = DP * 4 * BACK
    eye = one_hot(iota((32, 32), 0) == iota((32, 32), 1))
    place = dot(eye.astype(BF), routes[...].astype(F32).astype(BF), 1, 1)
    first, second = place[:, 0:1], place[:, 1:2]
    r = iota((32, cols), 1)
    c = (r & 15).astype(F32)
    owner = owner_of(r >> 6).astype(F32)
    hit = one_hot((first == owner) | (second == owner))
    before = one_hot(iota((32, 32), 1) < iota((32, 32), 0)).astype(BF)
    rank = dot(before, hit.astype(BF), 1, 0)
    paired = hit * one_hot(c < 10.0)
    both = jnp.concatenate(
        [paired * one_hot(rank == c), paired * one_hot(rank == c + 10.0)], axis=0
    )
    chosen[...] = both.astype(BF)
    lane = iota((32, 128), 1).astype(F32)
    for j in range(DP):
        owner_j = float(j // 4 if j < 8 else j - 6)
        here = one_hot(rank[:, 64 * j : 64 * j + 1] == lane)
        masks[0, j] = jnp.where(first == owner_j, here, 0.0)
        masks[1, j] = jnp.where(second == owner_j, here, 0.0)


def combine_kernel(chosen, masks, recv, grad_tokens, grad_probs):
    both = dot(chosen[...], recv[...].reshape(DP * 4 * BACK, 128), 1, 0)
    grad_tokens[...] = (both[0:32, 0:64] + both[32:64, 64:128]).astype(BF)
    sums = [jnp.zeros((32, 128), F32), jnp.zeros((32, 128), F32)]
    for j in range(DP):
        terms = jnp.sum(recv[j].astype(F32), axis=0)
        term = terms[10:11] + terms[11:12]
        for n in range(2):
            sums[n] += jnp.where(masks[n, j] > 0.5, term, 0.0)
    ones = jnp.ones((8, 128), F32)
    for n in range(2):
        row = dot(ones, sums[n], 1, 1, lax.Precision.HIGHEST)
        grad_probs[n : n + 1, :] = row[0:1, :]


def params(mib=16):
    return pltpu.CompilerParams(vmem_limit_bytes=mib * 1024 * 1024)


def shape(dims, dtype):
    return jax.ShapeDtypeStruct(dims, dtype)


def body(tokens, grad_out, routes, probs, gate_weight, up_weight, down_weight):
    any_space = pl.BlockSpec(memory_space=pl.ANY)
    smem = pl.BlockSpec(memory_space=pltpu.SMEM)
    core = lax.axis_index("core").astype(jnp.int32).reshape(1)
    routes_t = routes.T
    whole = [pl.BlockSpec(dims, lambda n: (0, 0)) for dims in ((2, 32), (32, 64))]
    picked = pl.pallas_call(
        select_kernel,
        grid=(1,),
        out_shape=pltpu.VMEM((DP, 4, ROWS, 128), BF),
        in_specs=[whole[0], whole[0], whole[1], whole[1]],
        out_specs=pl.BlockSpec((DP, 4, ROWS, 128), lambda n: (0, 0, 0, 0)),
        compiler_params=params(60),
        name="select_rows",
    )(routes_t, probs.T, tokens, grad_out)
    swap = [(0, 1), (1, 0)]
    w_own, w_away = pl.pallas_call(
        sort_kernel,
        out_shape=(pltpu.VMEM((336, 2048), BF),) * 2,
        in_specs=[smem] + [pl.BlockSpec(memory_space=pltpu.HBM)] * 3,
        out_specs=(VMEM,) * 2,
        scratch_shapes=[pltpu.VMEM((336, 4096), BF), pltpu.SemaphoreType.DMA((12,))],
        compiler_params=params(),
        cost_estimate=pl.CostEstimate(
            flops=0, bytes_accessed=8_000_000, transcendentals=0
        ),
        name="sort_columns",
    )(core, gate_weight, up_weight, down_weight)
    w_near = pl.pallas_call(
        hold_kernel,
        out_shape=pltpu.VMEM((336, 2048), BF),
        in_specs=[VMEM],
        out_specs=VMEM,
        compiler_params=params(),
        name="hold_columns",
    )(lax.ppermute(w_away, "core", swap))
    got = lax.all_to_all(picked.reshape(DP * 4, ROWS, 128), FAR, 0, 0, tiled=True)
    spread, prob = pl.pallas_call(
        spread_kernel,
        out_shape=(pltpu.HBM((8, 4, 128, SLOTS), BF), shape((1, SLOTS), F32)),
        in_specs=[VMEM],
        out_specs=(any_space, VMEM),
        scratch_shapes=[pltpu.VMEM((4, 128, SLOTS), BF), pltpu.SemaphoreType.DMA((32,))],
        compiler_params=params(),
        name="spread_rows",
    )(got.reshape(DP, 4, ROWS, 128))
    mine = lax.all_to_all(spread, PLANE, 0, 0, tiled=True)
    near = pl.pallas_call(
        near_kernel,
        out_shape=shape((336, SLOTS), F32),
        in_specs=[VMEM] * 2,
        out_specs=VMEM,
        compiler_params=params(),
        name="features_near",
    )(mine, w_near)
    part = pl.pallas_call(
        own_kernel,
        out_shape=shape((672, SLOTS), F32),
        in_specs=[VMEM] * 3,
        out_specs=VMEM,
        compiler_params=params(),
        name="features_own",
    )(mine, w_own, near)
    got_part = lax.ppermute(part, "core", swap)
    summed, pre = pl.pallas_call(
        grads_kernel,
        out_shape=(pltpu.HBM((8, 272, SLOTS), BF), pltpu.HBM((224, SLOTS), BF)),
        in_specs=[VMEM] * 5,
        out_specs=(any_space, any_space),
        scratch_shapes=[
            pltpu.VMEM((8, 272, SLOTS), BF),
            pltpu.VMEM((224, SLOTS), BF),
            pltpu.SemaphoreType.DMA((9,)),
        ],
        compiler_params=params(),
        name="hidden_and_input_grads",
    )(part, got_part, prob, w_own, w_near)
    parts = lax.all_to_all(summed, PLANE, 0, 0, tiled=True)
    back = pl.pallas_call(
        return_kernel,
        out_shape=pltpu.HBM((DP, 4, BACK, 128), BF),
        in_specs=[VMEM],
        out_specs=any_space,
        scratch_shapes=[pltpu.VMEM((4, DP, BACK, 128), BF), pltpu.SemaphoreType.DMA((4,))],
        compiler_params=params(),
        name="return_rows",
    )(parts)
    other = lax.ppermute(mine, "core", swap)
    grad_gate, grad_up, done = pl.pallas_call(
        weight_kernel,
        out_shape=(shape((112, 4096), BF),) * 2 + (shape((8, 128), F32),),
        in_specs=[smem, any_space, any_space, VMEM],
        out_specs=(VMEM,) * 3,
        scratch_shapes=[
            pltpu.VMEM((4, 8, 2, 64, SLOTS), BF),
            pltpu.SemaphoreType.DMA((16,)),
        ],
        compiler_params=params(),
        cost_estimate=pl.CostEstimate(
            flops=1_000, bytes_accessed=1_000, transcendentals=0
        ),
        name="weight_grads",
    )(core, mine, other, pre)
    home = lax.all_to_all(back.reshape(DP * 4, BACK, 128), FAR, 0, 0, tiled=True)
    chosen, masks = pl.pallas_call(
        mask_kernel,
        out_shape=(shape((64, DP * 4 * BACK), BF), shape((2, DP, 32, 128), F32)),
        in_specs=[VMEM] * 2,
        out_specs=(VMEM,) * 2,
        compiler_params=params(),
        name="masks",
    )(routes_t, done)
    grad_tokens, grad_probs = pl.pallas_call(
        combine_kernel,
        out_shape=(shape((32, 64), BF), shape((2, 32), F32)),
        in_specs=[VMEM] * 3,
        out_specs=(VMEM,) * 2,
        compiler_params=params(),
        name="combine",
    )(chosen, masks, home.reshape(DP, 4, BACK, 128))
    return grad_tokens, grad_probs.T, grad_gate, grad_up


def solution(mesh):
    fine = Mesh(mesh.devices.reshape(DP, 4, 2, 4, 2), ("dp", "yh", "yl", "x", "core"))
    hidden = ("yh", "yl", "x", "core")
    rows = P(("dp",) + hidden, None)
    placed = (P("dp", hidden), P("dp", hidden), P("dp", None), P("dp", None), rows, rows, rows)
    return jax.shard_map(
        body,
        mesh=fine,
        in_specs=placed,
        out_specs=(P("dp", hidden), P("dp", None), rows, rows),
        check_vma=False,
    )
```
